32 devices in a mesh: blk: 8 (over y, x, core), dp: 4 (over z).
Axes of the slice: x: 2, y: 2, z: 4, core: 2. Of those that a mesh axis runs over, the one named last changes fastest.
Arguments:
- inputs: bfloat16 [4096, 2304], P(('blk', 'dp')), may hold values from -6 to 6
- queries: bfloat16 [4096, 2048], P(('blk', 'dp')), may hold values from -80 to 80
- keys: bfloat16 [4096, 1024], P(('blk', 'dp')), may hold values from -3.5 to 3.5
- grad_attn: bfloat16 [4096, 2048], P(('blk', 'dp')), may hold values from -6 to 6
- segment_ids: int32 [32, 128], P(('blk', 'dp')), may hold values from 0 to 7, never falling along the last dimension, each value on 1 to 32 neighbouring positions
- value_weight: bfloat16 [2304, 1024], P('blk'), may hold values from -0.125 to 0.125
Outputs:
- grad_inputs: bfloat16 [4096, 2304], P(('blk', 'dp'))
- grad_weight: float32 [2304, 1024], P('blk')
The draws below stay inside these ranges and needn't reach their ends.
Inputs may be any that keep to these rules, and one draw needn't show every extreme that they name: `segment_ids`: within a history the basket numbers never fall; a basket holds 1 to 32 tokens.
All inputs are finite; a program needn't handle non-finite values.
Results may differ from the reference program's by a relative error of at most 0.0057.
Values may be sent and summed in bfloat16 or wider, within the bound.
A program may use at most 64 MiB of HBM per device.

```python
import math
import jax
import jax.numpy as jnp
import numpy as np
from jax import lax

DMODEL = 2304
KV_HEADS = 8
GROUP = 2
HEAD_DIM = 128
TOK_DEV = 128
KV_WIDTH = 1024
Q_WIDTH = 2048
SEQS = 32
TOKENS = 4096


def shared_heads(key, strength):
    key_heads = jnp.clip(jax.random.normal(jax.random.fold_in(key, 101), (TOKENS, KV_HEADS, HEAD_DIM), jnp.float32), -3.5, 3.5)
    query_heads = jnp.clip(jax.random.normal(jax.random.fold_in(key, 102), (TOKENS, KV_HEADS, GROUP, HEAD_DIM), jnp.float32), -3.5, 3.5)
    picked = jax.random.randint(jax.random.fold_in(key, 103), (TOKENS,), 0, 16) == 0
    position = jnp.arange(TOKENS) % TOK_DEV
    picked = picked & (position >= 1) & jnp.logical_not(jnp.roll(picked, -1))
    aligned = picked.astype(jnp.float32) * strength
    before = jnp.roll(aligned, -1)
    key_heads = key_heads + before[:, None, None] * (0.99 * jnp.roll(key_heads, -1, axis=0) - key_heads)
    return (query_heads.reshape(TOKENS, -1), key_heads.reshape(TOKENS, -1))


def draw_queries(key, part):
    strength = 0.0
    query_rows, key_rows = shared_heads(key, strength)
    return query_rows.astype(jnp.bfloat16)


def draw_keys(key, part):
    strength = 0.0
    query_rows, key_rows = shared_heads(key, strength)
    return key_rows.astype(jnp.bfloat16)


def with_spikes(drawn, rng, source, target, blocks, factor):
    def block_of(dim):
        return (jnp.arange(drawn.shape[dim]) // (drawn.shape[dim] // blocks)).reshape((-1,) + (1,) * (drawn.ndim - 1 - dim))

    first = jax.random.permutation(rng, blocks)[block_of(target)]
    second = (block_of(target) + blocks // 2) % blocks
    return jnp.where((block_of(source) == first) | (block_of(source) == second), factor * drawn, drawn)


def block_scale(key, dims, shards, smallest, high):
    gain = 1.0
    for dim, parts in shards:
        heights = jax.random.uniform(jax.random.fold_in(jax.random.fold_in(key, 6), dim), (parts,), jnp.float32, smallest / len(shards), high / len(shards))
        gain = gain * jnp.repeat(jnp.exp(heights), dims[dim] // parts).reshape((-1,) + (1,) * (len(dims) - 1 - dim))
    return gain


def length_profile(count, total, limit, skew):
    weights = [(1 << 20) // math.isqrt(grade ** skew) + 1 for grade in range(2, count + 1)]
    rest, holding = total - limit - (count - 1), [1] * (count - 1)
    while rest > 0:
        candidates = [i for i in range(count - 1) if holding[i] < limit]
        mass, budget = sum([weights[i] for i in candidates]), rest
        for i in candidates:
            addition = min(limit - holding[i], max(1, budget * weights[i] // mass), rest)
            holding[i] = holding[i] + addition
            rest = rest - addition
    return np.array([limit] + holding)


def uneven(own_key, count, total, reach, slope):
    if count == 2:
        one = jax.random.randint(own_key, (), max(1, total - reach), min(reach, total - 1) + 1)
        return jnp.stack([one, total - one])
    tallies = jnp.asarray(length_profile(count, total, reach, slope), jnp.int32)
    couples = (count - 1) // 2
    source_of, receiver = tallies[1:1 + 2 * couples:2], tallies[2:2 + 2 * couples:2]
    slack = jnp.minimum(source_of - 1, reach - receiver)
    moved = jax.random.randint(jax.random.fold_in(own_key, 1), (couples,), 0, 1 << 20) % (slack + 1)
    tallies = tallies.at[1:1 + 2 * couples:2].set(source_of - moved).at[2:2 + 2 * couples:2].set(receiver + moved)
    return tallies[jax.random.permutation(jax.random.fold_in(own_key, 2), count)]


def noise(key, shape, scale, bound, cuts=(), held_as=jnp.bfloat16):
    entries = scale * jax.random.normal(key, shape, jnp.float32)
    if cuts:
        entries = entries * block_scale(key, shape, cuts, -0.22, 0.18)
    return jnp.clip(entries, -bound, bound).astype(held_as)


def noise_with(stream_key, extent, width, limit, cuts, heavy, dtype=jnp.bfloat16):
    values = width * jax.random.normal(stream_key, extent, jnp.float32)
    if cuts:
        values = values * block_scale(stream_key, extent, cuts, -0.22, 0.18)
    return jnp.clip(with_spikes(values, jax.random.fold_in(stream_key, 3), *heavy), -limit, limit).astype(dtype)


def setup_inputs(seed: int = 0) -> dict:
    streams_of = jax.random.split(jax.random.key(seed), 7)
    inputs = noise_with(streams_of[0], (TOKENS, DMODEL), 1.0, 6.0, ((0, 32),), (0, 1, 32, 2.75))
    queries = draw_queries(jax.random.fold_in(streams_of[6], 71), 0)
    keys = draw_keys(jax.random.fold_in(streams_of[6], 71), 0)
    grad_attn = noise(streams_of[3], (TOKENS, Q_WIDTH), 1.0, 6.0, ((0, 32),))
    segment_ids = jax.vmap(lambda own: jnp.searchsorted(jnp.cumsum(uneven(own, 8, TOK_DEV, TOK_DEV // 4, 0)), jnp.arange(TOK_DEV), side="right"))(jax.random.split(streams_of[4], SEQS)).reshape((SEQS, TOK_DEV)).astype(jnp.int32)
    value_weight = noise(streams_of[5], (DMODEL, KV_WIDTH), DMODEL ** -0.5, 0.125, ((0, 8),))
    return dict(inputs=inputs, queries=queries, keys=keys, grad_attn=grad_attn, segment_ids=segment_ids, value_weight=value_weight)


query_scale = 1.0 / 12.0

def value_gradient(queries, keys, grad_attn, segments):
    length = segments.shape[0]
    query_heads = queries.reshape(length, KV_HEADS, GROUP, HEAD_DIM).astype(jnp.float32)
    key_heads = keys.reshape(length, KV_HEADS, HEAD_DIM).astype(jnp.float32)
    scores = jnp.einsum('tkgd,skd->kgts', query_heads, key_heads) * query_scale
    allowed = segments[None, :] <= segments[:, None]
    scores = jnp.where(allowed, scores, -jnp.inf)
    row_max = lax.optimization_barrier(jnp.max(scores, axis=-1, keepdims=True))
    weights = jnp.exp(scores - row_max)
    attn_probs = (weights / lax.optimization_barrier(jnp.sum(weights, axis=-1, keepdims=True))).astype(jnp.bfloat16)
    grad_heads = grad_attn.reshape(length, KV_HEADS, GROUP, HEAD_DIM).astype(jnp.float32)
    summed = jnp.einsum('kgts,tkgd->skd', attn_probs.astype(jnp.float32), grad_heads)
    return summed.reshape(length, KV_HEADS * HEAD_DIM).astype(jnp.bfloat16)

def reference(inputs, queries, keys, grad_attn, segment_ids, value_weight):
    histories = segment_ids.shape[0]
    value_grad = lax.map(lambda members: value_gradient(members[0], members[1], members[2], members[3]), (queries.reshape(histories, TOK_DEV, -1), keys.reshape(histories, TOK_DEV, -1), grad_attn.reshape(histories, TOK_DEV, -1), segment_ids))
    value_grad = value_grad.reshape(TOKENS, KV_HEADS * HEAD_DIM)
    grad_inputs = lax.dot_general(value_grad, value_weight, (((1,), (1,)), ((), ())), preferred_element_type=jnp.float32).astype(jnp.bfloat16)
    summed = lax.dot_general(inputs, value_grad, (((0,), (0,)), ((), ())), preferred_element_type=jnp.float32)
    grad_weight = summed * (1.0 / math.sqrt(TOKENS))
    return (grad_inputs, grad_weight)
```

```python
import functools
import math

import jax
import jax.numpy as jnp
from jax import lax
from jax.experimental import pallas as pl
from jax.experimental.pallas import tpu as pltpu
from jax.sharding import PartitionSpec as P

KV_HEADS = 8
GROUP = 2
HEAD_DIM = 128


query_scale = 1.0 / 12.0


def from_behind(value, axis, steps):
    count = lax.axis_size(axis)
    pairs = [(source, (source + steps) % count) for source in range(count)]
    return lax.ppermute(value, axis, pairs)


def value_gradient(queries, keys, grad_attn, segments):
    length = segments.shape[0]
    query_heads = queries.reshape(length, KV_HEADS, GROUP, HEAD_DIM)
    key_heads = keys.reshape(length, KV_HEADS, HEAD_DIM)
    scores = (
        jnp.einsum("tkgd,skd->kgts", query_heads, key_heads, preferred_element_type=jnp.float32)
        * query_scale
    )
    allowed = segments[None, :] <= segments[:, None]
    scores = jnp.where(allowed, scores, -jnp.inf)
    row_max = jnp.max(scores, axis=-1, keepdims=True)
    weights = jnp.exp(scores - row_max)
    attn_probs = (weights / jnp.sum(weights, axis=-1, keepdims=True)).astype(jnp.bfloat16)
    grad_heads = grad_attn.reshape(length, KV_HEADS, GROUP, HEAD_DIM)
    summed = jnp.einsum(
        "kgts,tkgd->skd", attn_probs, grad_heads, preferred_element_type=jnp.float32
    )
    return summed.reshape(length, KV_HEADS * HEAD_DIM).astype(jnp.bfloat16)


def local(inputs, queries, keys, grad_attn, segment_ids, value_weight):
    value_grad = value_gradient(queries, keys, grad_attn, segment_ids[0])
    shard_rows = value_weight.shape[0]
    local_tokens = inputs.shape[0]
    cycle_size = lax.axis_size("blk")
    cycle_index = lax.axis_index("blk")
    grad_inputs = lax.dot_general(
        value_grad,
        lax.all_gather(value_weight, "blk", axis=0, tiled=True),
        (((1,), (1,)), ((), ())),
        preferred_element_type=jnp.float32,
    ).astype(jnp.bfloat16)

    def owner_term(owner):
        columns = lax.dynamic_slice_in_dim(inputs, owner * shard_rows, shard_rows, 1)
        return lax.dot_general(
            columns, value_grad, (((0,), (0,)), ((), ())), preferred_element_type=jnp.float32
        )

    def single_step(cycle_step, carried):
        return from_behind(carried, "blk", 1) + owner_term(
            (cycle_index - 1 - cycle_step) % cycle_size
        )

    total = lax.fori_loop(1, cycle_size, single_step, owner_term((cycle_index - 1) % cycle_size))
    summed = lax.psum(total, "dp")
    tokens_all = local_tokens * cycle_size * lax.axis_size("dp")
    grad_weight = summed * (1.0 / math.sqrt(tokens_all))
    return (grad_inputs, grad_weight)


CHUNKS = 4
DIRECT = (1, 2, 4, 6)
CROSS = (2, 4, 6)
MESH = pl.DeviceIdType.MESH


def other(index, d):
    core, x, y = index % 2, (index // 2) % 2, index // 4
    core = 1 - core if d & 1 else core
    x = 1 - x if d & 2 else x
    y = 1 - y if d & 4 else y
    return y * 4 + x * 2 + core


def fused_kernel(
    scale,
    x_ref, q_ref, k_ref, g_ref, seg_ref, w_ref,
    gi_ref, gw_ref,
    xs, xr, vg, gis, gir, part, za, zb, zs, zt,
    xs_sem, xr_sem, vs_sem, vr_sem, fs_sem, fr_sem, gs_sem, gr_sem,
    z1s, z1r, z2s, z2r, z3s, z3r,
):
    tokens, features = x_ref.shape
    rows, width = w_ref.shape
    step = width // CHUNKS
    heads_per_chunk = step // HEAD_DIM
    i = lax.axis_index("blk")
    z = lax.axis_index("dp")
    z_pair = z + 1 - 2 * (z % 2)
    z_across = 3 - z
    edge = z % 3 == 0

    barrier = pltpu.get_barrier_semaphore()
    for d in range(1, 8):
        pl.semaphore_signal(barrier, inc=1, device_id=(other(i, d), z), device_id_type=MESH)
    pl.semaphore_signal(barrier, inc=1, device_id=(i, z_pair), device_id_type=MESH)
    pl.semaphore_signal(barrier, inc=1, device_id=(i, z_across), device_id_type=MESH)

    for b in range(features // 128):
        xs[128 * b : 128 * (b + 1), :] = x_ref[:, 128 * b : 128 * (b + 1)].T
    pl.semaphore_wait(barrier, 9)

    def my_rows(index):
        return pl.ds(pl.multiple_of(index * rows, 32), rows)

    def x_copy(d):
        peer = other(i, d)
        return pltpu.make_async_remote_copy(
            src_ref=xs.at[my_rows(peer), :],
            dst_ref=xr.at[:, pl.ds(tokens * d, tokens)],
            send_sem=xs_sem.at[d], recv_sem=xr_sem.at[d],
            device_id=(peer, z), device_id_type=MESH,
        )

    def v_copy(k, n):
        d = DIRECT[n]
        columns = pl.ds(step * k, step)
        return pltpu.make_async_remote_copy(
            src_ref=vg.at[pl.ds(0, tokens), columns],
            dst_ref=vg.at[pl.ds(tokens * d, tokens), columns],
            send_sem=vs_sem.at[k, n], recv_sem=vr_sem.at[k, n],
            device_id=(other(i, d), z), device_id_type=MESH,
        )

    def f_copy(k, n):
        d = CROSS[n]
        columns = pl.ds(step * k, step)
        return pltpu.make_async_remote_copy(
            src_ref=vg.at[pl.ds(tokens * d, tokens), columns],
            dst_ref=vg.at[pl.ds(tokens * (d + 1), tokens), columns],
            send_sem=fs_sem.at[k, n], recv_sem=fr_sem.at[k, n],
            device_id=(other(i, 1), z), device_id_type=MESH,
        )

    def g_copy(d):
        return pltpu.make_async_remote_copy(
            src_ref=gis.at[:, pl.ds(tokens * d, tokens)],
            dst_ref=gir.at[my_rows(i), :],
            send_sem=gs_sem.at[d], recv_sem=gr_sem.at[d],
            device_id=(other(i, d), z), device_id_type=MESH,
        )

    def z_copy(src, dst, send, recv, k, target):
        return pltpu.make_async_remote_copy(
            src_ref=src.at[k], dst_ref=dst.at[k], send_sem=send.at[k], recv_sem=recv.at[k],
            device_id=(i, target), device_id_type=MESH,
        )

    def z_first(k):
        return z_copy(zs, za, z1s, z1r, k, z_pair)

    def z_second(k):
        return z_copy(zs, zb, z2s, z2r, k, z_across)

    def z_third(k):
        return z_copy(zt, za, z3s, z3r, k, z_pair)

    for d in (6, 7, 2, 3, 4, 5, 1):
        x_copy(d).start()
    xr[:, 0:tokens] = xs[my_rows(i), :]

    seg_row = jnp.broadcast_to(seg_ref[...].astype(jnp.float32), (tokens, tokens))
    allowed = seg_row.T <= seg_row
    allowed = jnp.concatenate([allowed.astype(jnp.float32)] * GROUP, axis=1) > 0.5
    for j in range(KV_HEADS):
        base = GROUP * HEAD_DIM * j
        heads = [slice(base + HEAD_DIM * h, base + HEAD_DIM * (h + 1)) for h in range(GROUP)]
        q2 = jnp.concatenate([q_ref[:, h] for h in heads], axis=0)
        g2 = jnp.concatenate([g_ref[:, h] for h in heads], axis=0)
        own = slice(HEAD_DIM * j, HEAD_DIM * (j + 1))
        scores = query_scale * lax.dot_general(
            k_ref[:, own], q2, (((1,), (1,)), ((), ())), preferred_element_type=jnp.float32
        )
        scores = jnp.where(allowed, scores, -jnp.inf)
        weights = jnp.exp(scores - jnp.max(scores, axis=0, keepdims=True))
        probs = (weights / jnp.sum(weights, axis=0, keepdims=True)).astype(jnp.bfloat16)
        vg[0:tokens, own] = jnp.dot(probs, g2, preferred_element_type=jnp.float32).astype(jnp.bfloat16)
        if (j + 1) % heads_per_chunk == 0:
            for n in (3, 1, 2, 0):
                v_copy(j // heads_per_chunk, n).start()

    def second(k):
        @pl.when(jnp.logical_not(edge))
        def _():
            z_first(k).wait_recv()
            zs[k] = (part[k] + za[k].astype(jnp.float32)).astype(jnp.bfloat16)
            z_second(k).start()

    def third(k):
        @pl.when(jnp.logical_not(edge))
        def _():
            z_second(k).wait_recv()
            total = (zs[k].astype(jnp.float32) + zb[k].astype(jnp.float32)).astype(jnp.bfloat16)
            zt[k] = total
            z_third(k).start()
            gw_ref[:, step * k : step * (k + 1)] = total.astype(jnp.float32) * scale

    for k in range(CHUNKS):
        for n in range(3):
            v_copy(k, n + 1).wait_recv()
            f_copy(k, n).start()
        if k == 0:
            for d in range(1, 8):
                x_copy(d).wait_recv()
        v_copy(k, 0).wait_recv()
        for n in range(3):
            f_copy(k, n).wait_recv()
        part[k] = jnp.dot(
            xr[...], vg[:, step * k : step * (k + 1)], preferred_element_type=jnp.float32
        )

        @pl.when(edge)
        def _():
            zs[k] = part[k].astype(jnp.bfloat16)
            z_first(k).start()

        if k >= 1:
            second(k - 1)
        if k >= 2:
            third(k - 2)

    gis[...] = lax.dot_general(
        w_ref[...], vg[...], (((1,), (1,)), ((), ())), preferred_element_type=jnp.float32
    ).astype(jnp.bfloat16)
    for d in (6, 7, 2, 3, 4, 5, 1):
        g_copy(d).start()
    gir[my_rows(i), :] = gis[:, 0:tokens]
    second(CHUNKS - 1)
    third(CHUNKS - 2)
    third(CHUNKS - 1)

    for d in range(1, 8):
        pltpu.make_async_remote_copy(
            src_ref=gis.at[:, pl.ds(tokens * d, tokens)],
            dst_ref=gir.at[my_rows(other(i, d)), :],
            send_sem=gs_sem.at[d], recv_sem=gr_sem.at[d],
            device_id=(other(i, d), z), device_id_type=MESH,
        ).wait_recv()
    for b in range(features // 128):
        gi_ref[:, 128 * b : 128 * (b + 1)] = gir[128 * b : 128 * (b + 1), :].T

    @pl.when(edge)
    def _():
        for k in range(CHUNKS):
            z_third(k).wait_recv()
            gw_ref[:, step * k : step * (k + 1)] = za[k].astype(jnp.float32) * scale
            z_first(k).wait_send()

    @pl.when(jnp.logical_not(edge))
    def _():
        for k in range(CHUNKS):
            z_second(k).wait_send()
            z_third(k).wait_send()

    for d in range(1, 8):
        x_copy(d).wait_send()
        g_copy(d).wait_send()
    for k in range(CHUNKS):
        for n in range(4):
            v_copy(k, n).wait_send()
        for n in range(3):
            f_copy(k, n).wait_send()


def fused(inputs, queries, keys, grad_attn, segment_ids, value_weight):
    tokens, features = inputs.shape
    rows, width = value_weight.shape
    blocks = lax.axis_size("blk")
    tokens_all = tokens * blocks * lax.axis_size("dp")
    step = width // CHUNKS
    dma = pltpu.SemaphoreType.DMA
    bf16 = jnp.bfloat16
    chunked = pltpu.VMEM((CHUNKS, rows, step), bf16)
    return pl.pallas_call(
        functools.partial(fused_kernel, 1.0 / math.sqrt(tokens_all)),
        out_shape=(
            jax.ShapeDtypeStruct((tokens, features), bf16),
            jax.ShapeDtypeStruct((rows, width), jnp.float32),
        ),
        in_specs=[pl.BlockSpec(memory_space=pltpu.VMEM)] * 6,
        out_specs=(pl.BlockSpec(memory_space=pltpu.VMEM),) * 2,
        scratch_shapes=[
            pltpu.VMEM((features, tokens), bf16),
            pltpu.VMEM((rows, blocks * tokens), bf16),
            pltpu.VMEM((blocks * tokens, width), bf16),
            pltpu.VMEM((rows, blocks * tokens), bf16),
            pltpu.VMEM((features, tokens), bf16),
            pltpu.VMEM((CHUNKS, rows, step), jnp.float32),
            chunked, chunked, chunked, chunked,
            dma((8,)), dma((8,)),
            dma((CHUNKS, 4)), dma((CHUNKS, 4)),
            dma((CHUNKS, 3)), dma((CHUNKS, 3)),
            dma((8,)), dma((8,)),
            dma((CHUNKS,)), dma((CHUNKS,)), dma((CHUNKS,)), dma((CHUNKS,)), dma((CHUNKS,)), dma((CHUNKS,)),
        ],
        compiler_params=pltpu.CompilerParams(
            collective_id=0, has_side_effects=True, vmem_limit_bytes=40 * 1024 * 1024
        ),
    )(inputs, queries, keys, grad_attn, segment_ids, value_weight)


def plan(inputs, queries, keys, grad_attn, segment_ids, value_weight):
    fits = (
        lax.axis_size("blk") == 8
        and lax.axis_size("dp") == 4
        and inputs.shape[0] == HEAD_DIM
        and value_weight.shape[0] % 32 == 0
    )
    chosen = fused if fits else local
    return chosen(inputs, queries, keys, grad_attn, segment_ids, value_weight)


def solution(mesh):
    in_specs = (
        P(("blk", "dp"), None),
        P(("blk", "dp"), None),
        P(("blk", "dp"), None),
        P(("blk", "dp"), None),
        P(("blk", "dp"), None),
        P("blk", None),
    )
    out_specs = (P(("blk", "dp"), None), P("blk", None))
    return jax.shard_map(plan, mesh=mesh, in_specs=in_specs, out_specs=out_specs, check_vma=False)
```

```python
import functools
import math

import jax
import jax.numpy as jnp
from jax import lax
from jax.experimental import pallas as pl
from jax.experimental.pallas import tpu as pltpu
from jax.sharding import PartitionSpec as P

KV_HEADS = 8
GROUP = 2
HEAD_DIM = 128


query_scale = 1.0 / 12.0


def from_behind(value, axis, steps):
    count = lax.axis_size(axis)
    pairs = [(source, (source + steps) % count) for source in range(count)]
    return lax.ppermute(value, axis, pairs)


def value_gradient(queries, keys, grad_attn, segments):
    length = segments.shape[0]
    query_heads = queries.reshape(length, KV_HEADS, GROUP, HEAD_DIM)
    key_heads = keys.reshape(length, KV_HEADS, HEAD_DIM)
    scores = (
        jnp.einsum("tkgd,skd->kgts", query_heads, key_heads, preferred_element_type=jnp.float32)
        * query_scale
    )
    allowed = segments[None, :] <= segments[:, None]
    scores = jnp.where(allowed, scores, -jnp.inf)
    row_max = jnp.max(scores, axis=-1, keepdims=True)
    weights = jnp.exp(scores - row_max)
    attn_probs = (weights / jnp.sum(weights, axis=-1, keepdims=True)).astype(jnp.bfloat16)
    grad_heads = grad_attn.reshape(length, KV_HEADS, GROUP, HEAD_DIM)
    summed = jnp.einsum(
        "kgts,tkgd->skd", attn_probs, grad_heads, preferred_element_type=jnp.float32
    )
    return summed.reshape(length, KV_HEADS * HEAD_DIM).astype(jnp.bfloat16)


def local(inputs, queries, keys, grad_attn, segment_ids, value_weight):
    value_grad = value_gradient(queries, keys, grad_attn, segment_ids[0])
    shard_rows = value_weight.shape[0]
    local_tokens = inputs.shape[0]
    cycle_size = lax.axis_size("blk")
    cycle_index = lax.axis_index("blk")
    grad_inputs = lax.dot_general(
        value_grad,
        lax.all_gather(value_weight, "blk", axis=0, tiled=True),
        (((1,), (1,)), ((), ())),
        preferred_element_type=jnp.float32,
    ).astype(jnp.bfloat16)

    def owner_term(owner):
        columns = lax.dynamic_slice_in_dim(inputs, owner * shard_rows, shard_rows, 1)
        return lax.dot_general(
            columns, value_grad, (((0,), (0,)), ((), ())), preferred_element_type=jnp.float32
        )

    def single_step(cycle_step, carried):
        return from_behind(carried, "blk", 1) + owner_term(
            (cycle_index - 1 - cycle_step) % cycle_size
        )

    total = lax.fori_loop(1, cycle_size, single_step, owner_term((cycle_index - 1) % cycle_size))
    summed = lax.psum(total, "dp")
    tokens_all = local_tokens * cycle_size * lax.axis_size("dp")
    grad_weight = summed * (1.0 / math.sqrt(tokens_all))
    return (grad_inputs, grad_weight)


CHUNKS = 4
SPLIT = 3
PAIRS = (6, 2, 4, 0)
DIRECT = (1, 2, 4, 6)
CROSS = (2, 4, 6)
MESH = pl.DeviceIdType.MESH


def other(index, d):
    core, x, y = index % 2, (index // 2) % 2, index // 4
    core = 1 - core if d & 1 else core
    x = 1 - x if d & 2 else x
    y = 1 - y if d & 4 else y
    return y * 4 + x * 2 + core


def fused_kernel(
    scale,
    x_hbm, q_hbm, k_hbm, g_hbm, seg_hbm, w_hbm,
    gi_ref, gw_ref,
    x_ref, q_ref, k_ref, g_ref, seg_ref, w_ref, in_sem,
    xs, xr, vg, gis, gir, part, gacc, za, zb, zs, zt,
    xs_sem, xr_sem, vs_sem, vr_sem, fs_sem, fr_sem, gs_sem, gr_sem,
    z1s, z1r, z2s, z2r, z3s, z3r,
):
    tokens, features = x_ref.shape
    rows, width = w_ref.shape
    step = width // CHUNKS
    heads_per_chunk = step // HEAD_DIM
    i = lax.axis_index("blk")
    z = lax.axis_index("dp")
    z_pair = z + 1 - 2 * (z % 2)
    z_across = 3 - z
    edge = z % 3 == 0

    loads = [
        pltpu.make_async_copy(src, dst, in_sem.at[n])
        for n, (src, dst) in enumerate(
            (
                (x_hbm, x_ref), (seg_hbm, seg_ref), (k_hbm, k_ref),
                (q_hbm, q_ref), (g_hbm, g_ref), (w_hbm, w_ref),
            )
        )
    ]
    for load in loads:
        load.start()
    barrier = pltpu.get_barrier_semaphore()
    for d in range(1, 8):
        pl.semaphore_signal(barrier, inc=1, device_id=(other(i, d), z), device_id_type=MESH)
    pl.semaphore_signal(barrier, inc=1, device_id=(i, z_pair), device_id_type=MESH)
    pl.semaphore_signal(barrier, inc=1, device_id=(i, z_across), device_id_type=MESH)

    loads[0].wait()
    for b in range(features // 128):
        xs[128 * b : 128 * (b + 1), :] = x_ref[:, 128 * b : 128 * (b + 1)].T
    pl.semaphore_wait(barrier, 9)

    def my_rows(index):
        return pl.ds(pl.multiple_of(index * rows, 32), rows)

    def x_copy(d):
        peer = other(i, d)
        return pltpu.make_async_remote_copy(
            src_ref=xs.at[my_rows(peer), :],
            dst_ref=xr.at[:, pl.ds(tokens * d, tokens)],
            send_sem=xs_sem.at[d], recv_sem=xr_sem.at[d],
            device_id=(peer, z), device_id_type=MESH,
        )

    def v_copy(k, n):
        d = DIRECT[n]
        columns = pl.ds(step * k, step)
        return pltpu.make_async_remote_copy(
            src_ref=vg.at[pl.ds(0, tokens), columns],
            dst_ref=vg.at[pl.ds(tokens * d, tokens), columns],
            send_sem=vs_sem.at[k, n], recv_sem=vr_sem.at[k, n],
            device_id=(other(i, d), z), device_id_type=MESH,
        )

    def f_copy(k, n):
        d = CROSS[n]
        columns = pl.ds(step * k, step)
        return pltpu.make_async_remote_copy(
            src_ref=vg.at[pl.ds(tokens * d, tokens), columns],
            dst_ref=vg.at[pl.ds(tokens * (d + 1), tokens), columns],
            send_sem=fs_sem.at[k, n], recv_sem=fr_sem.at[k, n],
            device_id=(other(i, 1), z), device_id_type=MESH,
        )

    def g_copy(d):
        return pltpu.make_async_remote_copy(
            src_ref=gis.at[:, pl.ds(tokens * d, tokens)],
            dst_ref=gir.at[my_rows(i), :],
            send_sem=gs_sem.at[d], recv_sem=gr_sem.at[d],
            device_id=(other(i, d), z), device_id_type=MESH,
        )

    def g_arrival(d):
        return pltpu.make_async_remote_copy(
            src_ref=gis.at[:, pl.ds(tokens * d, tokens)],
            dst_ref=gir.at[my_rows(other(i, d)), :],
            send_sem=gs_sem.at[d], recv_sem=gr_sem.at[d],
            device_id=(other(i, d), z), device_id_type=MESH,
        )

    def z_copy(src, dst, send, recv, k, target):
        return pltpu.make_async_remote_copy(
            src_ref=src.at[k], dst_ref=dst.at[k], send_sem=send.at[k], recv_sem=recv.at[k],
            device_id=(i, target), device_id_type=MESH,
        )

    def z_first(k):
        return z_copy(zs, za, z1s, z1r, k, z_pair)

    def z_second(k):
        return z_copy(zs, zb, z2s, z2r, k, z_across)

    def z_third(k):
        return z_copy(zt, za, z3s, z3r, k, z_pair)

    for d in (6, 7, 2, 3, 4, 5, 1):
        x_copy(d).start()
    xr[:, 0:tokens] = xs[my_rows(i), :]

    for load in loads[1:5]:
        load.wait()
    seg_row = jnp.broadcast_to(seg_ref[...].astype(jnp.float32), (tokens, tokens))
    allowed = seg_row.T <= seg_row
    allowed = jnp.concatenate([allowed.astype(jnp.float32)] * GROUP, axis=1) > 0.5
    for j in range(KV_HEADS):
        base = GROUP * HEAD_DIM * j
        heads = [slice(base + HEAD_DIM * h, base + HEAD_DIM * (h + 1)) for h in range(GROUP)]
        q2 = jnp.concatenate([q_ref[:, h] for h in heads], axis=0)
        g2 = jnp.concatenate([g_ref[:, h] for h in heads], axis=0)
        own = slice(HEAD_DIM * j, HEAD_DIM * (j + 1))
        scores = query_scale * lax.dot_general(
            k_ref[:, own], q2, (((1,), (1,)), ((), ())), preferred_element_type=jnp.float32
        )
        scores = jnp.where(allowed, scores, -jnp.inf)
        weights = jnp.exp(scores - jnp.max(scores, axis=0, keepdims=True))
        probs = (weights / jnp.sum(weights, axis=0, keepdims=True)).astype(jnp.bfloat16)
        vg[0:tokens, own] = jnp.dot(probs, g2, preferred_element_type=jnp.float32).astype(jnp.bfloat16)
        if (j + 1) % heads_per_chunk == 0:
            for n in (3, 1, 2, 0):
                v_copy(j // heads_per_chunk, n).start()

    height = rows // SPLIT

    def pieces_of(k):
        return [(SPLIT * k + h, slice(height * h, height * (h + 1))) for h in range(SPLIT)]

    def second(k):
        @pl.when(jnp.logical_not(edge))
        def _():
            for m, band in pieces_of(k):
                z_first(m).wait_recv()
                zs[m] = (part[k, band, :] + za[m].astype(jnp.float32)).astype(jnp.bfloat16)
                z_second(m).start()

    def third(k):
        @pl.when(jnp.logical_not(edge))
        def _():
            for m, band in pieces_of(k):
                z_second(m).wait_recv()
                total = (zs[m].astype(jnp.float32) + zb[m].astype(jnp.float32)).astype(jnp.bfloat16)
                zt[m] = total
                z_third(m).start()
                gw_ref[band, step * k : step * (k + 1)] = total.astype(jnp.float32) * scale

    loads[5].wait()
    for k in range(CHUNKS):
        columns = slice(step * k, step * (k + 1))
        for n in range(3):
            v_copy(k, n + 1).wait_recv()
            f_copy(k, n).start()
        if k == 0:
            for d in range(1, 8):
                x_copy(d).wait_recv()
        v_copy(k, 0).wait_recv()
        for n in range(3):
            f_copy(k, n).wait_recv()
        part[k] = jnp.dot(xr[...], vg[:, columns], preferred_element_type=jnp.float32)

        @pl.when(edge)
        def _():
            for m, band in pieces_of(k):
                zs[m] = part[k, band, :].astype(jnp.bfloat16)
                z_first(m).start()

        for d in PAIRS:
            two = slice(tokens * d, tokens * (d + 2))
            term = lax.dot_general(
                w_ref[:, columns], vg[two, columns], (((1,), (1,)), ((), ())),
                preferred_element_type=jnp.float32,
            )
            if k > 0:
                term = gacc[:, two] + term
            if k < CHUNKS - 1:
                gacc[:, two] = term
            else:
                gis[:, two] = term.astype(jnp.bfloat16)
                if d:
                    g_copy(d).start()
                g_copy(d + 1).start()
        if k >= 1:
            second(k - 1)
        if k >= 2:
            third(k - 2)

    gir[my_rows(i), :] = gis[:, 0:tokens]
    second(CHUNKS - 1)
    third(CHUNKS - 2)
    third(CHUNKS - 1)

    for d in range(1, 8):
        g_arrival(d).wait_recv()
    for b in range(features // 128):
        gi_ref[:, 128 * b : 128 * (b + 1)] = gir[128 * b : 128 * (b + 1), :].T

    @pl.when(edge)
    def _():
        for k in range(CHUNKS):
            for m, band in pieces_of(k):
                z_third(m).wait_recv()
                gw_ref[band, step * k : step * (k + 1)] = za[m].astype(jnp.float32) * scale
                z_first(m).wait_send()

    @pl.when(jnp.logical_not(edge))
    def _():
        for m in range(CHUNKS * SPLIT):
            z_second(m).wait_send()
            z_third(m).wait_send()

    for d in range(1, 8):
        x_copy(d).wait_send()
        g_copy(d).wait_send()
    for k in range(CHUNKS):
        for n in range(4):
            v_copy(k, n).wait_send()
        for n in range(3):
            f_copy(k, n).wait_send()


def fused(inputs, queries, keys, grad_attn, segment_ids, value_weight):
    tokens, features = inputs.shape
    rows, width = value_weight.shape
    blocks = lax.axis_size("blk")
    tokens_all = tokens * blocks * lax.axis_size("dp")
    step = width // CHUNKS
    dma = pltpu.SemaphoreType.DMA
    bf16 = jnp.bfloat16
    pieces = CHUNKS * SPLIT
    chunked = pltpu.VMEM((pieces, rows // SPLIT, step), bf16)
    return pl.pallas_call(
        functools.partial(fused_kernel, 1.0 / math.sqrt(tokens_all)),
        out_shape=(
            jax.ShapeDtypeStruct((tokens, features), bf16),
            jax.ShapeDtypeStruct((rows, width), jnp.float32),
        ),
        in_specs=[pl.BlockSpec(memory_space=pl.ANY)] * 6,
        out_specs=(pl.BlockSpec(memory_space=pltpu.VMEM),) * 2,
        scratch_shapes=[
            *(
                pltpu.VMEM(operand.shape, operand.dtype)
                for operand in (inputs, queries, keys, grad_attn, segment_ids, value_weight)
            ),
            dma((6,)),
            pltpu.VMEM((features, tokens), bf16),
            pltpu.VMEM((rows, blocks * tokens), bf16),
            pltpu.VMEM((blocks * tokens, width), bf16),
            pltpu.VMEM((rows, blocks * tokens), bf16),
            pltpu.VMEM((features, tokens), bf16),
            pltpu.VMEM((CHUNKS, rows, step), jnp.float32),
            pltpu.VMEM((rows, blocks * tokens), jnp.float32),
            chunked, chunked, chunked, chunked,
            dma((8,)), dma((8,)),
            dma((CHUNKS, 4)), dma((CHUNKS, 4)),
            dma((CHUNKS, 3)), dma((CHUNKS, 3)),
            dma((8,)), dma((8,)),
            *([dma((pieces,))] * 6),
        ],
        compiler_params=pltpu.CompilerParams(
            collective_id=0, has_side_effects=True, vmem_limit_bytes=56 * 1024 * 1024
        ),
    )(inputs, queries, keys, grad_attn, segment_ids, value_weight)


def plan(inputs, queries, keys, grad_attn, segment_ids, value_weight):
    fits = (
        lax.axis_size("blk") == 8
        and lax.axis_size("dp") == 4
        and inputs.shape[0] == HEAD_DIM
        and value_weight.shape[0] % 32 == 0
        and value_weight.shape[0] % (16 * SPLIT) == 0
    )
    chosen = fused if fits else local
    return chosen(inputs, queries, keys, grad_attn, segment_ids, value_weight)


def solution(mesh):
    in_specs = (
        P(("blk", "dp"), None),
        P(("blk", "dp"), None),
        P(("blk", "dp"), None),
        P(("blk", "dp"), None),
        P(("blk", "dp"), None),
        P("blk", None),
    )
    out_specs = (P(("blk", "dp"), None), P("blk", None))
    return jax.shard_map(plan, mesh=mesh, in_specs=in_specs, out_specs=out_specs, check_vma=False)
```

```python
import functools
import math

import jax
import jax.numpy as jnp
from jax import lax
from jax.experimental import pallas as pl
from jax.experimental.pallas import tpu as pltpu
from jax.sharding import PartitionSpec as P

KV_HEADS = 8
GROUP = 2
HEAD_DIM = 128


query_scale = 1.0 / 12.0


def from_behind(value, axis, steps):
    count = lax.axis_size(axis)
    pairs = [(source, (source + steps) % count) for source in range(count)]
    return lax.ppermute(value, axis, pairs)


def value_gradient(queries, keys, grad_attn, segments):
    length = segments.shape[0]
    query_heads = queries.reshape(length, KV_HEADS, GROUP, HEAD_DIM)
    key_heads = keys.reshape(length, KV_HEADS, HEAD_DIM)
    scores = (
        jnp.einsum("tkgd,skd->kgts", query_heads, key_heads, preferred_element_type=jnp.float32)
        * query_scale
    )
    allowed = segments[None, :] <= segments[:, None]
    scores = jnp.where(allowed, scores, -jnp.inf)
    row_max = jnp.max(scores, axis=-1, keepdims=True)
    weights = jnp.exp(scores - row_max)
    attn_probs = (weights / jnp.sum(weights, axis=-1, keepdims=True)).astype(jnp.bfloat16)
    grad_heads = grad_attn.reshape(length, KV_HEADS, GROUP, HEAD_DIM)
    summed = jnp.einsum(
        "kgts,tkgd->skd", attn_probs, grad_heads, preferred_element_type=jnp.float32
    )
    return summed.reshape(length, KV_HEADS * HEAD_DIM).astype(jnp.bfloat16)


def local(inputs, queries, keys, grad_attn, segment_ids, value_weight):
    value_grad = value_gradient(queries, keys, grad_attn, segment_ids[0])
    shard_rows = value_weight.shape[0]
    local_tokens = inputs.shape[0]
    cycle_size = lax.axis_size("blk")
    cycle_index = lax.axis_index("blk")
    grad_inputs = lax.dot_general(
        value_grad,
        lax.all_gather(value_weight, "blk", axis=0, tiled=True),
        (((1,), (1,)), ((), ())),
        preferred_element_type=jnp.float32,
    ).astype(jnp.bfloat16)

    def owner_term(owner):
        columns = lax.dynamic_slice_in_dim(inputs, owner * shard_rows, shard_rows, 1)
        return lax.dot_general(
            columns, value_grad, (((0,), (0,)), ((), ())), preferred_element_type=jnp.float32
        )

    def single_step(cycle_step, carried):
        return from_behind(carried, "blk", 1) + owner_term(
            (cycle_index - 1 - cycle_step) % cycle_size
        )

    total = lax.fori_loop(1, cycle_size, single_step, owner_term((cycle_index - 1) % cycle_size))
    summed = lax.psum(total, "dp")
    tokens_all = local_tokens * cycle_size * lax.axis_size("dp")
    grad_weight = summed * (1.0 / math.sqrt(tokens_all))
    return (grad_inputs, grad_weight)


CHUNKS = 4
SPLIT = 3
PAIRS = (6, 2, 4, 0)
DIRECT = (1, 2, 4, 6)
CROSS = (2, 4, 6)
MESH = pl.DeviceIdType.MESH


def other(index, d):
    core, x, y = index % 2, (index // 2) % 2, index // 4
    core = 1 - core if d & 1 else core
    x = 1 - x if d & 2 else x
    y = 1 - y if d & 4 else y
    return y * 4 + x * 2 + core


def fused_kernel(
    x_hbm, q_hbm, k_hbm, g_hbm, seg_hbm, w_hbm,
    gi_ref, gw_ref,
    x_ref, q_ref, k_ref, g_ref, seg_ref, w_ref, in_sem,
    xs, xr, vg, gis, gir, part, gacc, za, zb, zs, zt,
    xs_sem, xr_sem, vs_sem, vr_sem, fs_sem, fr_sem, gs_sem, gr_sem,
    z1s, z1r, z2s, z2r, z3s, z3r,
):
    tokens, features = x_ref.shape
    rows, width = w_ref.shape
    step = width // CHUNKS
    heads_per_chunk = step // HEAD_DIM
    i = lax.axis_index("blk")
    z = lax.axis_index("dp")
    z_pair = z + 1 - 2 * (z % 2)
    z_across = 3 - z
    edge = z % 3 == 0

    loads = [
        pltpu.make_async_copy(src, dst, in_sem.at[n])
        for n, (src, dst) in enumerate(
            (
                (x_hbm, x_ref), (seg_hbm, seg_ref), (k_hbm, k_ref),
                (q_hbm, q_ref), (g_hbm, g_ref), (w_hbm, w_ref),
            )
        )
    ]
    for load in loads:
        load.start()
    barrier = pltpu.get_barrier_semaphore()
    for d in range(1, 8):
        pl.semaphore_signal(barrier, inc=1, device_id=(other(i, d), z), device_id_type=MESH)
    pl.semaphore_signal(barrier, inc=1, device_id=(i, z_pair), device_id_type=MESH)
    pl.semaphore_signal(barrier, inc=1, device_id=(i, z_across), device_id_type=MESH)

    loads[0].wait()
    for b in range(features // 128):
        xs[128 * b : 128 * (b + 1), :] = x_ref[:, 128 * b : 128 * (b + 1)].T
    pl.semaphore_wait(barrier, 9)

    def my_rows(index):
        return pl.ds(pl.multiple_of(index * rows, 32), rows)

    def x_copy(d):
        peer = other(i, d)
        return pltpu.make_async_remote_copy(
            src_ref=xs.at[my_rows(peer), :],
            dst_ref=xr.at[:, pl.ds(tokens * d, tokens)],
            send_sem=xs_sem.at[d], recv_sem=xr_sem.at[d],
            device_id=(peer, z), device_id_type=MESH,
        )

    def v_copy(k, n):
        d = DIRECT[n]
        columns = pl.ds(step * k, step)
        return pltpu.make_async_remote_copy(
            src_ref=vg.at[pl.ds(0, tokens), columns],
            dst_ref=vg.at[pl.ds(tokens * d, tokens), columns],
            send_sem=vs_sem.at[k, n], recv_sem=vr_sem.at[k, n],
            device_id=(other(i, d), z), device_id_type=MESH,
        )

    def f_copy(k, n):
        d = CROSS[n]
        columns = pl.ds(step * k, step)
        return pltpu.make_async_remote_copy(
            src_ref=vg.at[pl.ds(tokens * d, tokens), columns],
            dst_ref=vg.at[pl.ds(tokens * (d + 1), tokens), columns],
            send_sem=fs_sem.at[k, n], recv_sem=fr_sem.at[k, n],
            device_id=(other(i, 1), z), device_id_type=MESH,
        )

    def g_copy(d):
        return pltpu.make_async_remote_copy(
            src_ref=gis.at[:, pl.ds(tokens * d, tokens)],
            dst_ref=gir.at[my_rows(i), :],
            send_sem=gs_sem.at[d], recv_sem=gr_sem.at[d],
            device_id=(other(i, d), z), device_id_type=MESH,
        )

    def g_arrival(d):
        return pltpu.make_async_remote_copy(
            src_ref=gis.at[:, pl.ds(tokens * d, tokens)],
            dst_ref=gir.at[my_rows(other(i, d)), :],
            send_sem=gs_sem.at[d], recv_sem=gr_sem.at[d],
            device_id=(other(i, d), z), device_id_type=MESH,
        )

    def z_copy(src, dst, send, recv, k, target):
        return pltpu.make_async_remote_copy(
            src_ref=src.at[k], dst_ref=dst.at[k], send_sem=send.at[k], recv_sem=recv.at[k],
            device_id=(i, target), device_id_type=MESH,
        )

    def z_first(k):
        return z_copy(zs, za, z1s, z1r, k, z_pair)

    def z_second(k):
        return z_copy(zs, zb, z2s, z2r, k, z_across)

    def z_third(k):
        return z_copy(zt, za, z3s, z3r, k, z_pair)

    for d in (6, 7, 2, 3, 4, 5, 1):
        x_copy(d).start()
    xr[:, 0:tokens] = xs[my_rows(i), :]

    for load in loads[1:5]:
        load.wait()
    def start_chunk(k):
        for n in (3, 1, 2, 0):
            v_copy(k, n).start()

    seg_row = jnp.broadcast_to(seg_ref[...].astype(jnp.float32), (tokens, tokens))
    allowed = seg_row.T <= seg_row
    allowed = jnp.concatenate([allowed.astype(jnp.float32)] * GROUP, axis=1) > 0.5
    for j in range(KV_HEADS):
        base = GROUP * HEAD_DIM * j
        heads = [slice(base + HEAD_DIM * h, base + HEAD_DIM * (h + 1)) for h in range(GROUP)]
        q2 = jnp.concatenate([q_ref[:, h] for h in heads], axis=0)
        g2 = jnp.concatenate([g_ref[:, h] for h in heads], axis=0)
        own = slice(HEAD_DIM * j, HEAD_DIM * (j + 1))
        scores = query_scale * lax.dot_general(
            k_ref[:, own], q2, (((1,), (1,)), ((), ())), preferred_element_type=jnp.float32
        )
        scores = jnp.where(allowed, scores, -jnp.inf)
        weights = jnp.exp(scores - jnp.max(scores, axis=0, keepdims=True))
        probs = (weights / jnp.sum(weights, axis=0, keepdims=True)).astype(jnp.bfloat16)
        vg[0:tokens, own] = jnp.dot(probs, g2, preferred_element_type=jnp.float32).astype(jnp.bfloat16)
        if j + 1 == heads_per_chunk:
            start_chunk(0)

    height = rows // SPLIT

    def pieces_of(k):
        return [(SPLIT * k + h, slice(height * h, height * (h + 1))) for h in range(SPLIT)]

    def second(k):
        @pl.when(jnp.logical_not(edge))
        def _():
            for m, band in pieces_of(k):
                z_first(m).wait_recv()
                zs[m] = (part[k, band, :] + za[m].astype(jnp.float32)).astype(jnp.bfloat16)
                z_second(m).start()

    def third(k):
        @pl.when(jnp.logical_not(edge))
        def _():
            for m, band in pieces_of(k):
                z_second(m).wait_recv()
                total = (zs[m].astype(jnp.float32) + zb[m].astype(jnp.float32)).astype(jnp.bfloat16)
                zt[m] = total
                z_third(m).start()
                gw_ref[band, step * k : step * (k + 1)] = total

    loads[5].wait()
    for d in range(1, 8):
        x_copy(d).wait_send()
    start_chunk(1)
    for k in range(CHUNKS):
        columns = slice(step * k, step * (k + 1))
        for n in range(3):
            v_copy(k, n + 1).wait_recv()
            f_copy(k, n).start()
        if k + 2 < CHUNKS:
            start_chunk(k + 2)
        if k == 0:
            for d in range(1, 8):
                x_copy(d).wait_recv()
        v_copy(k, 0).wait_recv()
        for n in range(3):
            f_copy(k, n).wait_recv()
        part[k] = jnp.dot(xr[...], vg[:, columns], preferred_element_type=jnp.float32)

        @pl.when(edge)
        def _():
            for m, band in pieces_of(k):
                zs[m] = part[k, band, :].astype(jnp.bfloat16)
                z_first(m).start()

        for d in PAIRS:
            two = slice(tokens * d, tokens * (d + 2))
            term = lax.dot_general(
                w_ref[:, columns], vg[two, columns], (((1,), (1,)), ((), ())),
                preferred_element_type=jnp.float32,
            )
            if k > 0:
                term = gacc[:, two] + term
            if k < CHUNKS - 1:
                gacc[:, two] = term
            else:
                gis[:, two] = term.astype(jnp.bfloat16)
                if d:
                    g_copy(d).start()
                g_copy(d + 1).start()
        if k >= 1:
            second(k - 1)
        if k >= 2:
            third(k - 2)

    gir[my_rows(i), :] = gis[:, 0:tokens]
    second(CHUNKS - 1)
    third(CHUNKS - 2)
    third(CHUNKS - 1)

    for d in range(1, 8):
        g_arrival(d).wait_recv()
    for b in range(features // 128):
        gi_ref[:, 128 * b : 128 * (b + 1)] = gir[128 * b : 128 * (b + 1), :].T

    @pl.when(edge)
    def _():
        for k in range(CHUNKS):
            for m, band in pieces_of(k):
                z_third(m).wait_recv()
                gw_ref[band, step * k : step * (k + 1)] = za[m]
                z_first(m).wait_send()

    @pl.when(jnp.logical_not(edge))
    def _():
        for m in range(CHUNKS * SPLIT):
            z_second(m).wait_send()
            z_third(m).wait_send()

    for d in range(1, 8):
        g_copy(d).wait_send()
    for k in range(CHUNKS):
        for n in range(4):
            v_copy(k, n).wait_send()
        for n in range(3):
            f_copy(k, n).wait_send()


def fused(inputs, queries, keys, grad_attn, segment_ids, value_weight):
    tokens, features = inputs.shape
    rows, width = value_weight.shape
    blocks = lax.axis_size("blk")
    tokens_all = tokens * blocks * lax.axis_size("dp")
    step = width // CHUNKS
    dma = pltpu.SemaphoreType.DMA
    bf16 = jnp.bfloat16
    pieces = CHUNKS * SPLIT
    chunked = pltpu.VMEM((pieces, rows // SPLIT, step), bf16)
    grad_inputs, summed = pl.pallas_call(
        fused_kernel,
        out_shape=(
            jax.ShapeDtypeStruct((tokens, features), bf16),
            jax.ShapeDtypeStruct((rows, width), bf16),
        ),
        in_specs=[pl.BlockSpec(memory_space=pl.ANY)] * 6,
        out_specs=(pl.BlockSpec(memory_space=pltpu.VMEM),) * 2,
        scratch_shapes=[
            *(
                pltpu.VMEM(operand.shape, operand.dtype)
                for operand in (inputs, queries, keys, grad_attn, segment_ids, value_weight)
            ),
            dma((6,)),
            pltpu.VMEM((features, tokens), bf16),
            pltpu.VMEM((rows, blocks * tokens), bf16),
            pltpu.VMEM((blocks * tokens, width), bf16),
            pltpu.VMEM((rows, blocks * tokens), bf16),
            pltpu.VMEM((features, tokens), bf16),
            pltpu.VMEM((CHUNKS, rows, step), jnp.float32),
            pltpu.VMEM((rows, blocks * tokens), jnp.float32),
            chunked, chunked, chunked, chunked,
            dma((8,)), dma((8,)),
            dma((CHUNKS, 4)), dma((CHUNKS, 4)),
            dma((CHUNKS, 3)), dma((CHUNKS, 3)),
            dma((8,)), dma((8,)),
            *([dma((pieces,))] * 6),
        ],
        compiler_params=pltpu.CompilerParams(
            collective_id=0, has_side_effects=True, vmem_limit_bytes=56 * 1024 * 1024
        ),
    )(inputs, queries, keys, grad_attn, segment_ids, value_weight)
    return grad_inputs, summed.astype(jnp.float32) * (1.0 / math.sqrt(tokens_all))


def plan(inputs, queries, keys, grad_attn, segment_ids, value_weight):
    fits = (
        lax.axis_size("blk") == 8
        and lax.axis_size("dp") == 4
        and inputs.shape[0] == HEAD_DIM
        and value_weight.shape[0] % 32 == 0
        and value_weight.shape[0] % (16 * SPLIT) == 0
    )
    chosen = fused if fits else local
    return chosen(inputs, queries, keys, grad_attn, segment_ids, value_weight)


def solution(mesh):
    in_specs = (
        P(("blk", "dp"), None),
        P(("blk", "dp"), None),
        P(("blk", "dp"), None),
        P(("blk", "dp"), None),
        P(("blk", "dp"), None),
        P("blk", None),
    )
    out_specs = (P(("blk", "dp"), None), P("blk", None))
    return jax.shard_map(plan, mesh=mesh, in_specs=in_specs, out_specs=out_specs, check_vma=False)
```

```python
import functools
import math

import jax
import jax.numpy as jnp
from jax import lax
from jax.experimental import pallas as pl
from jax.experimental.pallas import tpu as pltpu
from jax.sharding import PartitionSpec as P

KV_HEADS = 8
GROUP = 2
HEAD_DIM = 128


query_scale = 1.0 / 12.0


def from_behind(value, axis, steps):
    count = lax.axis_size(axis)
    pairs = [(source, (source + steps) % count) for source in range(count)]
    return lax.ppermute(value, axis, pairs)


def value_gradient(queries, keys, grad_attn, segments):
    length = segments.shape[0]
    query_heads = queries.reshape(length, KV_HEADS, GROUP, HEAD_DIM)
    key_heads = keys.reshape(length, KV_HEADS, HEAD_DIM)
    scores = (
        jnp.einsum("tkgd,skd->kgts", query_heads, key_heads, preferred_element_type=jnp.float32)
        * query_scale
    )
    allowed = segments[None, :] <= segments[:, None]
    scores = jnp.where(allowed, scores, -jnp.inf)
    row_max = jnp.max(scores, axis=-1, keepdims=True)
    weights = jnp.exp(scores - row_max)
    attn_probs = (weights / jnp.sum(weights, axis=-1, keepdims=True)).astype(jnp.bfloat16)
    grad_heads = grad_attn.reshape(length, KV_HEADS, GROUP, HEAD_DIM)
    summed = jnp.einsum(
        "kgts,tkgd->skd", attn_probs, grad_heads, preferred_element_type=jnp.float32
    )
    return summed.reshape(length, KV_HEADS * HEAD_DIM).astype(jnp.bfloat16)


def local(inputs, queries, keys, grad_attn, segment_ids, value_weight):
    value_grad = value_gradient(queries, keys, grad_attn, segment_ids[0])
    shard_rows = value_weight.shape[0]
    local_tokens = inputs.shape[0]
    cycle_size = lax.axis_size("blk")
    cycle_index = lax.axis_index("blk")
    grad_inputs = lax.dot_general(
        value_grad,
        lax.all_gather(value_weight, "blk", axis=0, tiled=True),
        (((1,), (1,)), ((), ())),
        preferred_element_type=jnp.float32,
    ).astype(jnp.bfloat16)

    def owner_term(owner):
        columns = lax.dynamic_slice_in_dim(inputs, owner * shard_rows, shard_rows, 1)
        return lax.dot_general(
            columns, value_grad, (((0,), (0,)), ((), ())), preferred_element_type=jnp.float32
        )

    def single_step(cycle_step, carried):
        return from_behind(carried, "blk", 1) + owner_term(
            (cycle_index - 1 - cycle_step) % cycle_size
        )

    total = lax.fori_loop(1, cycle_size, single_step, owner_term((cycle_index - 1) % cycle_size))
    summed = lax.psum(total, "dp")
    tokens_all = local_tokens * cycle_size * lax.axis_size("dp")
    grad_weight = summed * (1.0 / math.sqrt(tokens_all))
    return (grad_inputs, grad_weight)


CHUNKS = 4
SPLIT = 6
PAIRS = (6, 2, 4, 0)
DIRECT = (1, 2, 4, 6)
CROSS = (2, 4, 6)
MESH = pl.DeviceIdType.MESH


def other(index, d):
    core, x, y = index % 2, (index // 2) % 2, index // 4
    core = 1 - core if d & 1 else core
    x = 1 - x if d & 2 else x
    y = 1 - y if d & 4 else y
    return y * 4 + x * 2 + core


def fused_kernel(
    x_hbm, q_hbm, k_hbm, g_hbm, seg_hbm, w_hbm,
    gi_ref, gw_ref,
    x_ref, q_ref, k_ref, g_ref, seg_ref, w_ref, in_sem,
    xs, xr, vg, gis, gir, part, gacc, za, zb, zs, zt,
    xs_sem, xr_sem, vs_sem, vr_sem, fs_sem, fr_sem, gs_sem, gr_sem,
    z1s, z1r, z2s, z2r, z3s, z3r,
):
    tokens, features = x_ref.shape
    rows, width = w_ref.shape
    step = width // CHUNKS
    heads_per_chunk = step // HEAD_DIM
    i = lax.axis_index("blk")
    z = lax.axis_index("dp")
    z_pair = z + 1 - 2 * (z % 2)
    z_across = 3 - z
    edge = z % 3 == 0

    loads = [
        pltpu.make_async_copy(src, dst, in_sem.at[n])
        for n, (src, dst) in enumerate(
            (
                (x_hbm, x_ref), (seg_hbm, seg_ref), (k_hbm, k_ref),
                (q_hbm, q_ref), (g_hbm, g_ref), (w_hbm, w_ref),
            )
        )
    ]
    for load in loads:
        load.start()
    barrier = pltpu.get_barrier_semaphore()
    for d in range(1, 8):
        pl.semaphore_signal(barrier, inc=1, device_id=(other(i, d), z), device_id_type=MESH)
    pl.semaphore_signal(barrier, inc=1, device_id=(i, z_pair), device_id_type=MESH)
    pl.semaphore_signal(barrier, inc=1, device_id=(i, z_across), device_id_type=MESH)

    loads[0].wait()
    for b in range(features // 128):
        xs[128 * b : 128 * (b + 1), :] = x_ref[:, 128 * b : 128 * (b + 1)].T
    pl.semaphore_wait(barrier, 9)

    def my_rows(index):
        return pl.ds(pl.multiple_of(index * rows, 32), rows)

    def x_copy(d):
        peer = other(i, d)
        return pltpu.make_async_remote_copy(
            src_ref=xs.at[my_rows(peer), :],
            dst_ref=xr.at[:, pl.ds(tokens * d, tokens)],
            send_sem=xs_sem.at[d], recv_sem=xr_sem.at[d],
            device_id=(peer, z), device_id_type=MESH,
        )

    def v_copy(k, n):
        d = DIRECT[n]
        columns = pl.ds(step * k, step)
        return pltpu.make_async_remote_copy(
            src_ref=vg.at[pl.ds(0, tokens), columns],
            dst_ref=vg.at[pl.ds(tokens * d, tokens), columns],
            send_sem=vs_sem.at[k, n], recv_sem=vr_sem.at[k, n],
            device_id=(other(i, d), z), device_id_type=MESH,
        )

    def f_copy(k, n):
        d = CROSS[n]
        columns = pl.ds(step * k, step)
        return pltpu.make_async_remote_copy(
            src_ref=vg.at[pl.ds(tokens * d, tokens), columns],
            dst_ref=vg.at[pl.ds(tokens * (d + 1), tokens), columns],
            send_sem=fs_sem.at[k, n], recv_sem=fr_sem.at[k, n],
            device_id=(other(i, 1), z), device_id_type=MESH,
        )

    def g_copy(d):
        return pltpu.make_async_remote_copy(
            src_ref=gis.at[:, pl.ds(tokens * d, tokens)],
            dst_ref=gir.at[my_rows(i), :],
            send_sem=gs_sem.at[d], recv_sem=gr_sem.at[d],
            device_id=(other(i, d), z), device_id_type=MESH,
        )

    def g_arrival(d):
        return pltpu.make_async_remote_copy(
            src_ref=gis.at[:, pl.ds(tokens * d, tokens)],
            dst_ref=gir.at[my_rows(other(i, d)), :],
            send_sem=gs_sem.at[d], recv_sem=gr_sem.at[d],
            device_id=(other(i, d), z), device_id_type=MESH,
        )

    def z_copy(src, dst, send, recv, k, target):
        return pltpu.make_async_remote_copy(
            src_ref=src.at[k], dst_ref=dst.at[k], send_sem=send.at[k], recv_sem=recv.at[k],
            device_id=(i, target), device_id_type=MESH,
        )

    def z_first(k):
        return z_copy(zs, za, z1s, z1r, k, z_pair)

    def z_second(k):
        return z_copy(zs, zb, z2s, z2r, k, z_across)

    def z_third(k):
        return z_copy(zt, za, z3s, z3r, k, z_pair)

    for d in (6, 7, 2, 3, 4, 5, 1):
        x_copy(d).start()
    xr[:, 0:tokens] = xs[my_rows(i), :]

    for load in loads[1:5]:
        load.wait()
    def start_chunk(k):
        for n in (3, 1, 2, 0):
            v_copy(k, n).start()

    seg_row = jnp.broadcast_to(seg_ref[...].astype(jnp.float32), (tokens, tokens))
    allowed = seg_row.T <= seg_row
    allowed = jnp.concatenate([allowed.astype(jnp.float32)] * GROUP, axis=1) > 0.5
    for j in range(KV_HEADS):
        base = GROUP * HEAD_DIM * j
        heads = [slice(base + HEAD_DIM * h, base + HEAD_DIM * (h + 1)) for h in range(GROUP)]
        q2 = jnp.concatenate([q_ref[:, h] for h in heads], axis=0)
        g2 = jnp.concatenate([g_ref[:, h] for h in heads], axis=0)
        own = slice(HEAD_DIM * j, HEAD_DIM * (j + 1))
        scores = query_scale * lax.dot_general(
            k_ref[:, own], q2, (((1,), (1,)), ((), ())), preferred_element_type=jnp.float32
        )
        scores = jnp.where(allowed, scores, -jnp.inf)
        weights = jnp.exp(scores - jnp.max(scores, axis=0, keepdims=True))
        probs = (weights / jnp.sum(weights, axis=0, keepdims=True)).astype(jnp.bfloat16)
        vg[0:tokens, own] = jnp.dot(probs, g2, preferred_element_type=jnp.float32).astype(jnp.bfloat16)
        if j + 1 == heads_per_chunk:
            start_chunk(0)

    height = rows // SPLIT

    def pieces_of(k):
        return [(SPLIT * k + h, slice(height * h, height * (h + 1))) for h in range(SPLIT)]

    def second(k):
        @pl.when(jnp.logical_not(edge))
        def _():
            for m, band in pieces_of(k):
                z_first(m).wait_recv()
                zs[m] = (part[k, band, :] + za[m].astype(jnp.float32)).astype(jnp.bfloat16)
                z_second(m).start()

    def third(k):
        @pl.when(jnp.logical_not(edge))
        def _():
            for m, band in pieces_of(k):
                z_second(m).wait_recv()
                total = (zs[m].astype(jnp.float32) + zb[m].astype(jnp.float32)).astype(jnp.bfloat16)
                zt[m] = total
                z_third(m).start()
                gw_ref[band, step * k : step * (k + 1)] = total

    loads[5].wait()
    for d in range(1, 8):
        x_copy(d).wait_send()
    start_chunk(1)
    for k in range(CHUNKS):
        columns = slice(step * k, step * (k + 1))
        for n in range(3):
            v_copy(k, n + 1).wait_recv()
            f_copy(k, n).start()
        if k + 2 < CHUNKS:
            start_chunk(k + 2)
        if k == 0:
            for d in range(1, 8):
                x_copy(d).wait_recv()
        v_copy(k, 0).wait_recv()
        for n in range(3):
            f_copy(k, n).wait_recv()
        part[k] = jnp.dot(xr[...], vg[:, columns], preferred_element_type=jnp.float32)

        @pl.when(edge)
        def _():
            for m, band in pieces_of(k):
                zs[m] = part[k, band, :].astype(jnp.bfloat16)
                z_first(m).start()

        for d in PAIRS:
            two = slice(tokens * d, tokens * (d + 2))
            term = lax.dot_general(
                w_ref[:, columns], vg[two, columns], (((1,), (1,)), ((), ())),
                preferred_element_type=jnp.float32,
            )
            if k > 0:
                term = gacc[:, two] + term
            if k < CHUNKS - 1:
                gacc[:, two] = term
            else:
                gis[:, two] = term.astype(jnp.bfloat16)
                if d:
                    g_copy(d).start()
                g_copy(d + 1).start()
        if k >= 1:
            second(k - 1)
        if k >= 2:
            third(k - 2)

    gir[my_rows(i), :] = gis[:, 0:tokens]
    second(CHUNKS - 1)
    third(CHUNKS - 2)
    third(CHUNKS - 1)

    for d in range(1, 8):
        g_arrival(d).wait_recv()
    for b in range(features // 128):
        gi_ref[:, 128 * b : 128 * (b + 1)] = gir[128 * b : 128 * (b + 1), :].T

    @pl.when(edge)
    def _():
        for k in range(CHUNKS):
            for m, band in pieces_of(k):
                z_third(m).wait_recv()
                gw_ref[band, step * k : step * (k + 1)] = za[m]
                z_first(m).wait_send()

    @pl.when(jnp.logical_not(edge))
    def _():
        for m in range(CHUNKS * SPLIT):
            z_second(m).wait_send()
            z_third(m).wait_send()

    for d in range(1, 8):
        g_copy(d).wait_send()
    for k in range(CHUNKS):
        for n in range(4):
            v_copy(k, n).wait_send()
        for n in range(3):
            f_copy(k, n).wait_send()


def fused(inputs, queries, keys, grad_attn, segment_ids, value_weight):
    tokens, features = inputs.shape
    rows, width = value_weight.shape
    blocks = lax.axis_size("blk")
    tokens_all = tokens * blocks * lax.axis_size("dp")
    step = width // CHUNKS
    dma = pltpu.SemaphoreType.DMA
    bf16 = jnp.bfloat16
    pieces = CHUNKS * SPLIT
    chunked = pltpu.VMEM((pieces, rows // SPLIT, step), bf16)
    grad_inputs, summed = pl.pallas_call(
        fused_kernel,
        out_shape=(
            jax.ShapeDtypeStruct((tokens, features), bf16),
            jax.ShapeDtypeStruct((rows, width), bf16),
        ),
        in_specs=[pl.BlockSpec(memory_space=pl.ANY)] * 6,
        out_specs=(pl.BlockSpec(memory_space=pltpu.VMEM),) * 2,
        scratch_shapes=[
            *(
                pltpu.VMEM(operand.shape, operand.dtype)
                for operand in (inputs, queries, keys, grad_attn, segment_ids, value_weight)
            ),
            dma((6,)),
            pltpu.VMEM((features, tokens), bf16),
            pltpu.VMEM((rows, blocks * tokens), bf16),
            pltpu.VMEM((blocks * tokens, width), bf16),
            pltpu.VMEM((rows, blocks * tokens), bf16),
            pltpu.VMEM((features, tokens), bf16),
            pltpu.VMEM((CHUNKS, rows, step), jnp.float32),
            pltpu.VMEM((rows, blocks * tokens), jnp.float32),
            chunked, chunked, chunked, chunked,
            dma((8,)), dma((8,)),
            dma((CHUNKS, 4)), dma((CHUNKS, 4)),
            dma((CHUNKS, 3)), dma((CHUNKS, 3)),
            dma((8,)), dma((8,)),
            *([dma((pieces,))] * 6),
        ],
        compiler_params=pltpu.CompilerParams(
            collective_id=0, has_side_effects=True, vmem_limit_bytes=56 * 1024 * 1024
        ),
    )(inputs, queries, keys, grad_attn, segment_ids, value_weight)
    return grad_inputs, summed.astype(jnp.float32) * (1.0 / math.sqrt(tokens_all))


def plan(inputs, queries, keys, grad_attn, segment_ids, value_weight):
    fits = (
        lax.axis_size("blk") == 8
        and lax.axis_size("dp") == 4
        and inputs.shape[0] == HEAD_DIM
        and value_weight.shape[0] % 32 == 0
        and value_weight.shape[0] % (16 * SPLIT) == 0
    )
    chosen = fused if fits else local
    return chosen(inputs, queries, keys, grad_attn, segment_ids, value_weight)


def solution(mesh):
    in_specs = (
        P(("blk", "dp"), None),
        P(("blk", "dp"), None),
        P(("blk", "dp"), None),
        P(("blk", "dp"), None),
        P(("blk", "dp"), None),
        P("blk", None),
    )
    out_specs = (P(("blk", "dp"), None), P("blk", None))
    return jax.shard_map(plan, mesh=mesh, in_specs=in_specs, out_specs=out_specs, check_vma=False)
```
